128 devices in a mesh: ctx: 16 (over y, x), head: 8 (over z, core).
Axes of the slice: x: 4, y: 4, z: 4, core: 2. Of those that a mesh axis runs over, the one named last changes fastest.
Arguments:
- queries: bfloat16 [32768, 4096], P(('ctx', 'head')), may hold values from -26 to 26
- span_kv: bfloat16 [32768, 2048], P(('ctx', 'head')), may hold values from -6 to 6
- context_kv: bfloat16 [8, 262144, 256], P('head', 'ctx'), may hold values from -6 to 6
- selected: int32 [8, 64, 3], P('head'), may hold values from 0 to 511, as said below
Outputs:
- attended: bfloat16 [32768, 4096], P(('ctx', 'head'))
The draws below stay inside these ranges and needn't reach their ends.
Inputs may be any that keep to these rules, and one draw needn't show every extreme that they name: `selected`: within one query block the 3 indices differ. For each key-value head and each run of 4 query blocks that one index of ctx holds, at most 2 of their selections lie in one range of 32 context blocks that one index of ctx holds, and exactly 2 in some range.
All inputs are finite; a program needn't handle non-finite values.
Results may differ from the reference program's by a relative error of at most 0.0057.
Values may be sent and summed in bfloat16 or wider, within the bound.
No kernel may reach another device: no remote copies, remote signals or barrier semaphores. Data moves between devices by JAX's collectives and lax.ppermute only.
A program may use at most 192 MiB of HBM per device.

```python
import jax
import jax.numpy as jnp
from jax import lax

DH = 128
GROUP = 4
BLK = 512
TOPK = 3
CAP = 2
QB_DEV = 4
KVB_DEV = 32
KV_HEADS = 8
HEADS = 32
QBLOCKS = 64
QTOK = 32768
CONTEXT = 262144


def draw_queries(key, part):
    key = jax.random.fold_in(key, 11)
    base_key = jax.random.fold_in(key, 0)
    shape = (QTOK, HEADS * DH)
    values = jnp.clip(jax.random.normal(base_key, shape, jnp.float32), -6.0, 6.0)
    return values.astype(jnp.bfloat16)


def draw_context_kv(key, part):
    key = jax.random.fold_in(key, 12)
    shape = (KV_HEADS, CONTEXT, 2 * DH)
    values = jnp.clip(jax.random.normal(key, shape, jnp.float32), -6.0, 6.0)
    return values.astype(jnp.bfloat16)


def draw_span_kv(key, part):
    key = jax.random.fold_in(key, 14)
    shape = (QTOK, KV_HEADS * 2 * DH)
    values = jnp.clip(jax.random.normal(key, shape, jnp.float32), -6.0, 6.0)
    return values.astype(jnp.bfloat16)


def draw_selected(key, part):
    key = jax.random.fold_in(key, 13)
    ctx_count = QBLOCKS // QB_DEV
    place_count = ctx_count * CAP
    entry_count = QB_DEV * TOPK

    def one_group(group_key):
        keys_list = jax.random.split(group_key, 5)
        place_index = jnp.arange(place_count, dtype=jnp.int32)
        holder_lookup = place_index // CAP
        copy_of = place_index % CAP
        popularity = jax.random.permutation(keys_list[0], ctx_count)
        popular_holder = (popularity < max(1, ctx_count // 4)).astype(jnp.int32)
        favored_holder = jax.random.randint(keys_list[1], (), 0, ctx_count)
        random_jitter = jax.random.randint(keys_list[2], (place_count,), 0, 1 << 16)
        extra_score = popular_holder[holder_lookup] * (1 << 15) + (holder_lookup == favored_holder).astype(jnp.int32) * (1 << 17)
        gate_score = (random_jitter + extra_score) * place_count + place_index
        unused, chosen = lax.top_k(gate_score, entry_count)
        layouts = jax.vmap(lambda one_key: jax.random.permutation(one_key, KVB_DEV))(jax.random.split(keys_list[3], ctx_count))
        local_block = layouts[holder_lookup, copy_of].astype(jnp.int32)
        block_of = holder_lookup * KVB_DEV + local_block
        picked = block_of[chosen]
        shuffled = picked[jax.random.permutation(keys_list[4], entry_count)]
        return shuffled.reshape(QB_DEV, TOPK)
    groups = jax.vmap(one_group)(jax.random.split(key, KV_HEADS * ctx_count))
    return groups.reshape(KV_HEADS, QBLOCKS, TOPK).astype(jnp.int32)


def setup_inputs(seed: int = 0) -> dict:
    streams_of = jax.random.split(jax.random.key(seed), 5)
    return {
        "queries": draw_queries(jax.random.fold_in(streams_of[4], 71), 0),
        "span_kv": draw_span_kv(jax.random.fold_in(streams_of[4], 71), 0),
        "context_kv": draw_context_kv(jax.random.fold_in(streams_of[4], 71), 0),
        "selected": draw_selected(jax.random.fold_in(streams_of[4], 71), 0),
    }


def block_partial(query_tile, key_tile, value_tile, visible):
    group_heads = query_tile.shape[1] // DH
    query_f32 = query_tile.reshape(BLK, group_heads, DH).astype(jnp.float32)
    key_f32 = key_tile.astype(jnp.float32)
    value_f32 = value_tile.astype(jnp.float32)
    scores = jnp.einsum('qgd,kd->gqk', query_f32, key_f32) * (DH ** -0.5)
    scores = jnp.where(visible[None], scores, -jnp.inf)
    maximum = jnp.max(scores, axis=-1, keepdims=True)
    exponent = jnp.exp(scores - maximum)
    totals = jnp.sum(exponent, axis=-1, keepdims=True)
    rounded = lax.optimization_barrier((exponent / totals).astype(jnp.bfloat16))
    weights = rounded.astype(jnp.float32)
    partial_out = jnp.einsum('gqk,kd->qgd', weights, value_f32).astype(jnp.bfloat16)
    block_stat = maximum[..., 0] + jnp.log(totals[..., 0])
    return partial_out.reshape(BLK, group_heads * DH), block_stat


def merge_blocks(partials, block_stats):
    count = partials.shape[0]
    peak_stat = jnp.max(block_stats, axis=0, keepdims=True)
    total_stat = peak_stat + jnp.log(jnp.sum(jnp.exp(block_stats - peak_stat), axis=0, keepdims=True))
    factors = jnp.exp(block_stats - total_stat)
    values = partials.astype(jnp.float32).reshape(count, BLK, GROUP, DH)
    scaled = jnp.swapaxes(factors, 1, 2)[..., None] * values
    return jnp.sum(scaled, axis=0).astype(jnp.bfloat16).reshape(BLK, GROUP * DH)


def reference(queries, span_kv, context_kv, selected):
    row_index = jnp.arange(BLK, dtype=jnp.int32)
    causal_keep = row_index[:, None] >= row_index[None, :]
    everything = jnp.ones((BLK, BLK), dtype=bool)

    def one_head(head_index):
        head_queries = lax.dynamic_slice_in_dim(queries, (head_index * (GROUP * DH)).astype(jnp.int32), GROUP * DH, 1)
        head_span = lax.dynamic_slice_in_dim(span_kv, (head_index * (2 * DH)).astype(jnp.int32), 2 * DH, 1)
        head_context = lax.dynamic_index_in_dim(context_kv, head_index, 0, keepdims=False)
        head_picks = lax.dynamic_index_in_dim(selected, head_index, 0, keepdims=False)

        def one_block(block_index):
            start = (block_index * BLK).astype(jnp.int32)
            query_tile = lax.dynamic_slice_in_dim(head_queries, start, BLK, 0)
            own_tile = lax.dynamic_slice_in_dim(head_span, start, BLK, 0)
            picks_row = lax.dynamic_index_in_dim(head_picks, block_index, 0, keepdims=False)
            outs_list = []
            stat_list = []
            for rank in range(TOPK):
                first = (picks_row[rank] * BLK).astype(jnp.int32)
                far_tile = lax.dynamic_slice_in_dim(head_context, first, BLK, 0)
                part_out, part_stat = block_partial(query_tile, far_tile[:, :DH], far_tile[:, DH:], everything)
                outs_list.append(part_out)
                stat_list.append(part_stat)
            part_out, part_stat = block_partial(query_tile, own_tile[:, :DH], own_tile[:, DH:], causal_keep)
            outs_list.append(part_out)
            stat_list.append(part_stat)
            return merge_blocks(jnp.stack(outs_list), jnp.stack(stat_list))

        return lax.map(one_block, jnp.arange(QBLOCKS, dtype=jnp.int32))

    result = lax.map(one_head, jnp.arange(KV_HEADS, dtype=jnp.int32))
    return jnp.transpose(result, (1, 2, 0, 3)).reshape(QTOK, KV_HEADS * GROUP * DH)
```

```python
import jax
import jax.numpy as jnp
import numpy as np
from jax import lax
from jax.experimental import pallas as pl
from jax.experimental.pallas import tpu as pltpu
from jax.sharding import PartitionSpec as P

BLK = 512
CAP = 2
DH = 128
GROUP = 4
TOPK = 3
QB = 4
ENTRIES = QB * TOPK
SIDE = 4
ONES = 16
C = DH ** -0.5 * 1.4426950408889634

ORDER = [
    (0, 1), (0, 3), (1, 0), (3, 0), (2, 2), (1, 1), (3, 3), (1, 3),
    (3, 1), (1, 2), (3, 2), (2, 1), (2, 3), (0, 2), (2, 0),
]
SELF = len(ORDER)
FIRST = 5
GROUPS = [[SELF] + list(range(0, 5)), list(range(5, 9)), list(range(9, 13))]
LAST = [13, 14]

VMEM = pl.BlockSpec(memory_space=pltpu.VMEM)
SMEM = pl.BlockSpec(memory_space=pltpu.SMEM)
ANY = pl.BlockSpec(memory_space=pl.ANY)
PARAMS = pltpu.CompilerParams(vmem_limit_bytes=32 * 1024 * 1024)


def place_table(members):
    table = np.full((SIDE * SIDE,), -1, np.int32)
    for place, number in enumerate(members):
        dy, dx = (0, 0) if number == SELF else ORDER[number]
        table[dy * SIDE + dx] = place
    return jnp.asarray(table)


def ctx_position():
    rank = lax.axis_index("ctx")
    return rank // SIDE, rank % SIDE


def serve_kernel(members, sel_ref, tiles_ref, *refs):
    outs, sem = refs[:-1], refs[-1]
    y, x = ctx_position()
    me = y * SIDE + x
    copies = []
    for out, number in zip(outs, members):
        dy, dx = (0, 0) if number == SELF else ORDER[number]
        asker = ((y + dy) % SIDE) * SIDE + (x + dx) % SIDE
        found = jnp.int32(0)
        which = [jnp.int32(0)] * CAP
        for e in range(ENTRIES):
            pick = sel_ref[asker * QB + e // TOPK, e % TOPK]
            hit = pick // 32 == me
            for s in range(CAP):
                which[s] = jnp.where(hit & (found == s), pick % 32, which[s])
            found = found + hit.astype(jnp.int32)
        for s in range(CAP):
            copy = pltpu.make_async_copy(tiles_ref.at[which[s]], out.at[s], sem.at[len(copies)])
            copy.start()
            copies.append(copy)
    for copy in copies:
        copy.wait()


def serve_call(members, sel, tiles):
    n = len(members)
    return pl.pallas_call(
        lambda *refs: serve_kernel(members, *refs),
        in_specs=[SMEM, ANY],
        out_specs=[VMEM] * n,
        out_shape=[jax.ShapeDtypeStruct((CAP, BLK, 2 * DH), tiles.dtype)] * n,
        scratch_shapes=[pltpu.SemaphoreType.DMA((CAP * n,))],
        compiler_params=PARAMS,
        name="serve",
    )(sel, tiles)


def pack_kernel(heads, q_ref, s_ref, out_ref, sem):
    width = GROUP * DH
    copies = []
    for h in range(heads):
        copies.append(
            pltpu.make_async_copy(
                q_ref.at[:, pl.ds(h * width, width)], out_ref.at[h, :, pl.ds(0, width)], sem.at[2 * h]
            )
        )
        copies.append(
            pltpu.make_async_copy(
                s_ref.at[:, pl.ds(h * 2 * DH, 2 * DH)], out_ref.at[h, :, pl.ds(width, 2 * DH)], sem.at[2 * h + 1]
            )
        )
    for copy in copies:
        copy.start()
    for copy in copies:
        copy.wait()


def pack_call(queries, span_kv, heads):
    rows = queries.shape[0]
    return pl.pallas_call(
        lambda *refs: pack_kernel(heads, *refs),
        in_specs=[ANY, ANY],
        out_specs=VMEM,
        out_shape=jax.ShapeDtypeStruct((heads, rows, (GROUP + 2) * DH), queries.dtype),
        scratch_shapes=[pltpu.SemaphoreType.DMA((2 * heads,))],
        compiler_params=PARAMS,
        name="pack",
    )(queries, span_kv)


def values_t(v):
    return jnp.concatenate([v.T, jnp.ones((ONES, BLK), v.dtype)], axis=0)


def scores_t(k, q):
    return lax.dot_general(k, q, (((1,), (1,)), ((), ())), preferred_element_type=jnp.float32)


def own_kernel(x_ref, acc, ml):
    def body(b, carry):
        k = x_ref[b, :, GROUP * DH:(GROUP + 1) * DH]
        vt = values_t(x_ref[b, :, (GROUP + 1) * DH:])
        key = lax.broadcasted_iota(jnp.int32, (BLK, BLK), 0)
        query = lax.broadcasted_iota(jnp.int32, (BLK, BLK), 1)
        found = [scores_t(k, x_ref[b, :, g * DH:(g + 1) * DH]) for g in range(GROUP)]
        for g in range(GROUP):
            s = jnp.where(key <= query, found[g], -jnp.inf)
            m = jnp.max(s, axis=0, keepdims=True)
            p = jnp.exp2((s - m) * C).astype(jnp.bfloat16)
            pv = jnp.dot(vt, p, preferred_element_type=jnp.float32)
            acc[b, g] = pv[:DH]
            ml[b, g, 0:1] = m
            ml[b, g, 1:2] = pv[DH:DH + 1]
        return carry

    lax.fori_loop(0, QB, body, 0)


def add_block(q, kv, acc, ml, at):
    k = kv[:, :DH]
    vt = values_t(kv[:, DH:])
    found = [scores_t(k, q[:, g * DH:(g + 1) * DH]) for g in range(GROUP)]
    for g in range(GROUP):
        s = found[g]
        m_old = ml[at, g, 0:1]
        m = jnp.maximum(m_old, jnp.max(s, axis=0, keepdims=True))
        p = jnp.exp2((s - m) * C).astype(jnp.bfloat16)
        alpha = jnp.exp2((m_old - m) * C)
        pv = jnp.dot(vt, p, preferred_element_type=jnp.float32)
        acc[at, g] = acc[at, g] * alpha + pv[:DH]
        ml[at, g, 0:1] = m
        ml[at, g, 1:2] = ml[at, g, 1:2] * alpha + pv[DH:DH + 1]


def each_arrived(sel_ref, place_ref, x_ref, kv_refs, q_s, kv_s, first, count, step):
    y, x = ctx_position()
    base = (y * SIDE + x) * QB

    def body(e, carry):
        pick = sel_ref[base + e // TOPK, e % TOPK]
        owner = pick // 32

        def earlier(f, n):
            same = sel_ref[base + f // TOPK, f % TOPK] // 32 == owner
            return n + same.astype(jnp.int32)

        slot = lax.fori_loop(0, e, earlier, jnp.int32(0))
        dy = (y - owner // SIDE + SIDE) % SIDE
        dx = (x - owner % SIDE + SIDE) % SIDE
        place = place_ref[dy * SIDE + dx]
        for i, ref in enumerate(kv_refs):
            @pl.when(place == i)
            def _(ref=ref):
                kv_s[...] = ref[slot]

        @pl.when(place >= 0)
        def _():
            q_s[...] = x_ref[e // TOPK, :, :GROUP * DH]
            step(e // TOPK)

        return carry

    lax.fori_loop(first, first + count, body, 0)


def far_kernel(n, sel_ref, place_ref, x_ref, *refs):
    kv_refs, (acc_in, ml_in, acc, ml, q_s, kv_s) = refs[:n], refs[n:]
    each_arrived(
        sel_ref, place_ref, x_ref, kv_refs, q_s, kv_s, 0, ENTRIES,
        lambda b: add_block(q_s, kv_s[...], acc, ml, b),
    )


def last_kernel(n, ahead, sel_ref, place_ref, x_ref, *refs):
    kv_refs, (acc_in, ml_in, same_ref, other_ref, acc, ml, q_s, kv_s, out_s) = refs[:n], refs[n:]
    rank = lax.axis_index("head")
    b = (rank // 2 + ahead) % QB
    core = rank % 2
    acc[0] = acc_in[b]
    ml[0] = ml_in[b]
    each_arrived(
        sel_ref, place_ref, x_ref, kv_refs, q_s, kv_s, b * TOPK, TOPK,
        lambda b: add_block(q_s, kv_s[...], acc, ml, 0),
    )
    for g in range(GROUP):
        out = acc[0, g] / ml[0, g, 1:2]
        out_s[:, g * DH:(g + 1) * DH] = out.T.astype(out_s.dtype)
    half = BLK // 2
    same_ref[...] = out_s[pl.ds(pl.multiple_of(core * half, half), half), :]
    other_ref[...] = out_s[pl.ds(pl.multiple_of((1 - core) * half, half), half), :]


ACC = (QB, GROUP, DH, BLK)
ML = (QB, GROUP, 8, BLK)


def state_shapes():
    return [jax.ShapeDtypeStruct(ACC, jnp.float32), jax.ShapeDtypeStruct(ML, jnp.float32)]


def cost(blocks):
    units = int(blocks * GROUP)
    return pl.CostEstimate(
        flops=units * 4 * BLK * BLK * DH, bytes_accessed=units * BLK * DH * 2, transcendentals=units * BLK * BLK
    )


def own_call(x):
    return pl.pallas_call(
        own_kernel,
        in_specs=[VMEM],
        out_specs=[VMEM, VMEM],
        out_shape=state_shapes(),
        compiler_params=PARAMS,
        cost_estimate=cost(QB),
        name="own_blocks",
    )(x)


def far_call(sel, place, x, tiles, acc, ml):
    n = len(tiles)
    return pl.pallas_call(
        lambda *refs: far_kernel(n, *refs),
        in_specs=[SMEM, SMEM] + [VMEM] * (n + 3),
        out_specs=[VMEM, VMEM],
        out_shape=state_shapes(),
        scratch_shapes=[pltpu.VMEM((BLK, GROUP * DH), x.dtype), pltpu.VMEM((BLK, 2 * DH), x.dtype)],
        input_output_aliases={n + 3: 0, n + 4: 1},
        compiler_params=PARAMS,
        cost_estimate=cost(n * 0.75),
        name="far_blocks",
    )(sel, place, x, *tiles, acc, ml)


def last_call(ahead, sel, place, x, tiles, acc, ml):
    n = len(tiles)
    half = BLK // 2
    return pl.pallas_call(
        lambda *refs: last_kernel(n, ahead, *refs),
        in_specs=[SMEM, SMEM] + [VMEM] * (n + 3),
        out_specs=[VMEM, VMEM],
        out_shape=[jax.ShapeDtypeStruct((half, GROUP * DH), x.dtype)] * 2,
        scratch_shapes=[
            pltpu.VMEM((1,) + ACC[1:], jnp.float32),
            pltpu.VMEM((1,) + ML[1:], jnp.float32),
            pltpu.VMEM((BLK, GROUP * DH), x.dtype),
            pltpu.VMEM((BLK, 2 * DH), x.dtype),
            pltpu.VMEM((BLK, GROUP * DH), x.dtype),
        ],
        compiler_params=PARAMS,
        cost_estimate=cost(1),
        name="last_blocks",
    )(sel, place, x, *tiles, acc, ml)


def assemble_kernel(steps, *refs):
    pieces, out_ref = refs[:-1], refs[-1]
    rank = lax.axis_index("head")
    z, core = rank // 2, rank % 2
    width = GROUP * DH
    for (dz, dc), piece in zip(steps, pieces):
        sender = ((z - dz + QB) % QB) * 2 + (core + dc) % 2
        out_ref[:, pl.ds(pl.multiple_of(sender * width, width), width)] = piece[...]


def assemble_call(steps, pieces, heads):
    rows, width = pieces[0].shape
    return pl.pallas_call(
        lambda *refs: assemble_kernel(steps, *refs),
        in_specs=[VMEM] * len(pieces),
        out_specs=VMEM,
        out_shape=jax.ShapeDtypeStruct((rows, heads * width), pieces[0].dtype),
        compiler_params=PARAMS,
        name="assemble",
    )(*pieces)


def ctx_shift(value, dy, dx):
    pairs = [
        (y * SIDE + x, ((y + dy) % SIDE) * SIDE + (x + dx) % SIDE) for y in range(SIDE) for x in range(SIDE)
    ]
    return lax.ppermute(value, "ctx", pairs)


def head_shift(value, dz, dc):
    pairs = [(z * 2 + c, ((z + dz) % QB) * 2 + (c + dc) % 2) for z in range(QB) for c in range(2)]
    return lax.ppermute(value, "head", pairs)


def local(queries, span_kv, context_kv, selected):
    heads = lax.axis_size("head")
    rows = queries.shape[0]
    sel = selected[0]
    stored = context_kv[0]
    tiles = stored.reshape(stored.shape[0] // BLK, BLK, 2 * DH)

    numbers = list(range(SELF + 1))
    sent = dict(zip(numbers[:FIRST], serve_call(numbers[:FIRST], sel, tiles)))
    sent.update(zip(numbers[FIRST:], serve_call(numbers[FIRST:], sel, tiles)))
    packed = pack_call(queries, span_kv, heads)

    arrived = {SELF: sent[SELF]}
    for number, (dy, dx) in enumerate(ORDER):
        arrived[number] = ctx_shift(sent[number], dy, dx)
    x = lax.all_to_all(packed, "head", split_axis=0, concat_axis=0, tiled=True)
    x = x.reshape(QB, heads * rows // QB, (GROUP + 2) * DH)

    acc, ml = own_call(x)
    for members in GROUPS:
        acc, ml = far_call(sel, place_table(members), x, [arrived[i] for i in members], acc, ml)

    steps, pieces = [], []
    for dz in (2, 1, 3, 0):
        same, other = last_call(dz, sel, place_table(LAST), x, [arrived[i] for i in LAST], acc, ml)
        for dc, piece in ((0, same), (1, other)):
            steps.append((dz, dc))
            pieces.append(head_shift(piece, dz, dc) if dz or dc else piece)
    return assemble_call(steps, pieces, heads)


def solution(mesh):
    placed = (
        P(("ctx", "head"), None),
        P(("ctx", "head"), None),
        P("head", "ctx", None),
        P("head", None, None),
    )
    return jax.shard_map(
        local, mesh=mesh, in_specs=placed, out_specs=P(("ctx", "head"), None), check_vma=False
    )
```

```python
import jax
import jax.numpy as jnp
import numpy as np
from jax import lax
from jax.experimental import pallas as pl
from jax.experimental.pallas import tpu as pltpu
from jax.sharding import PartitionSpec as P

BLK = 512
CAP = 2
DH = 128
GROUP = 4
TOPK = 3
QB = 4
ENTRIES = QB * TOPK
SIDE = 4
ONES = 16
C = DH ** -0.5 * 1.4426950408889634

ORDER = [
    (0, 1), (0, 3), (1, 0), (3, 0), (2, 2), (1, 1), (3, 3), (1, 3),
    (3, 1), (1, 2), (3, 2), (2, 1), (2, 3), (0, 2), (2, 0),
]
SELF = len(ORDER)
FIRST = 5
GROUPS = [[SELF, 0, 1, 2, 3, 4], [5, 6, 7, 8, 9], [10, 11]]
LAST = [12, 13, 14]
FLIGHT = 5

VMEM = pl.BlockSpec(memory_space=pltpu.VMEM)
SMEM = pl.BlockSpec(memory_space=pltpu.SMEM)
HBM = pl.BlockSpec(memory_space=pltpu.HBM)
WIDE = pltpu.CompilerParams(vmem_limit_bytes=56 * 1024 * 1024)
PARAMS = pltpu.CompilerParams(vmem_limit_bytes=20 * 1024 * 1024)


def place_table(members):
    table = np.full((SIDE * SIDE,), -1, np.int32)
    for place, number in enumerate(members):
        dy, dx = (0, 0) if number == SELF else ORDER[number]
        table[dy * SIDE + dx] = place
    return jnp.asarray(table)


def ctx_position():
    rank = lax.axis_index("ctx")
    return rank // SIDE, rank % SIDE


def serve_kernel(members, sel_ref, tiles_ref, *refs):
    outs, (stage, sem, sem_out) = refs[:-3], refs[-3:]
    y, x = ctx_position()
    me = y * SIDE + x
    copies = []
    for out, number in zip(outs, members):
        dy, dx = (0, 0) if number == SELF else ORDER[number]
        asker = ((y + dy) % SIDE) * SIDE + (x + dx) % SIDE
        found = jnp.int32(0)
        which = [jnp.int32(0)] * CAP
        for e in range(ENTRIES):
            pick = sel_ref[asker * QB + e // TOPK, e % TOPK]
            hit = pick // 32 == me
            for s in range(CAP):
                which[s] = jnp.where(hit & (found == s), pick % 32, which[s])
            found = found + hit.astype(jnp.int32)
        for s in range(CAP):
            place = len(copies)
            copy = pltpu.make_async_copy(tiles_ref.at[which[s]], stage.at[place], sem.at[place])
            copy.start()
            copies.append((copy, pltpu.make_async_copy(stage.at[place], out.at[s], sem_out.at[place])))
    for copy, onward in copies:
        copy.wait()
        onward.start()
    for _, onward in copies:
        onward.wait()


def serve_call(members, sel, tiles):
    n = len(members)
    return pl.pallas_call(
        lambda *refs: serve_kernel(members, *refs),
        in_specs=[SMEM, HBM],
        out_specs=[HBM] * n,
        out_shape=[jax.ShapeDtypeStruct((CAP, BLK, 2 * DH), tiles.dtype)] * n,
        scratch_shapes=[
            pltpu.VMEM((CAP * n, BLK, 2 * DH), tiles.dtype),
            pltpu.SemaphoreType.DMA((CAP * n,)),
            pltpu.SemaphoreType.DMA((CAP * n,)),
        ],
        compiler_params=WIDE,
        name="serve",
    )(sel, tiles)


def pack_kernel(heads, q_ref, s_ref, out_ref, stage, sem, sem_out):
    width = GROUP * DH
    copies = []
    for h in range(heads):
        copies.append(
            pltpu.make_async_copy(
                q_ref.at[:, pl.ds(h * width, width)], stage.at[h, :, pl.ds(0, width)], sem.at[2 * h]
            )
        )
        copies.append(
            pltpu.make_async_copy(
                s_ref.at[:, pl.ds(h * 2 * DH, 2 * DH)], stage.at[h, :, pl.ds(width, 2 * DH)], sem.at[2 * h + 1]
            )
        )
    for copy in copies:
        copy.start()
    onward = []
    for h in range(heads):
        copies[2 * h].wait()
        copies[2 * h + 1].wait()
        onward.append(pltpu.make_async_copy(stage.at[h], out_ref.at[h], sem_out.at[h]))
        onward[h].start()
    for copy in onward:
        copy.wait()


def pack_call(queries, span_kv, heads):
    rows = queries.shape[0]
    return pl.pallas_call(
        lambda *refs: pack_kernel(heads, *refs),
        in_specs=[HBM, HBM],
        out_specs=HBM,
        out_shape=jax.ShapeDtypeStruct((heads, rows, (GROUP + 2) * DH), queries.dtype),
        scratch_shapes=[
            pltpu.VMEM((heads, rows, (GROUP + 2) * DH), queries.dtype),
            pltpu.SemaphoreType.DMA((2 * heads,)),
            pltpu.SemaphoreType.DMA((heads,)),
        ],
        compiler_params=WIDE,
        name="pack",
    )(queries, span_kv)


def values_t(v):
    return jnp.concatenate([v.T, jnp.ones((ONES, BLK), v.dtype)], axis=0)


def scores_t(k, q):
    return lax.dot_general(k, q, (((1,), (1,)), ((), ())), preferred_element_type=jnp.float32)


def own_kernel(x_ref, acc, ml):
    def body(b, carry):
        k = x_ref[b, :, GROUP * DH:(GROUP + 1) * DH]
        vt = values_t(x_ref[b, :, (GROUP + 1) * DH:])
        key = lax.broadcasted_iota(jnp.int32, (BLK, BLK), 0)
        query = lax.broadcasted_iota(jnp.int32, (BLK, BLK), 1)
        found = [scores_t(k, x_ref[b, :, g * DH:(g + 1) * DH]) for g in range(GROUP)]
        for g in range(GROUP):
            s = jnp.where(key <= query, found[g], -jnp.inf)
            m = jnp.max(s, axis=0, keepdims=True)
            p = jnp.exp2((s - m) * C).astype(jnp.bfloat16)
            pv = jnp.dot(vt, p, preferred_element_type=jnp.float32)
            acc[b, g] = pv[:DH]
            ml[b, g, 0:1] = m
            ml[b, g, 1:2] = pv[DH:DH + 1]
        return carry

    lax.fori_loop(0, QB, body, 0)


def add_block(q, kv, acc, ml, at):
    k = kv[:, :DH]
    vt = values_t(kv[:, DH:])
    found = [scores_t(k, q[:, g * DH:(g + 1) * DH]) for g in range(GROUP)]
    for g in range(GROUP):
        s = found[g]
        m_old = ml[at, g, 0:1]
        m = jnp.maximum(m_old, jnp.max(s, axis=0, keepdims=True))
        p = jnp.exp2((s - m) * C).astype(jnp.bfloat16)
        alpha = jnp.exp2((m_old - m) * C)
        pv = jnp.dot(vt, p, preferred_element_type=jnp.float32)
        acc[at, g] = acc[at, g] * alpha + pv[:DH]
        ml[at, g, 0:1] = m
        ml[at, g, 1:2] = ml[at, g, 1:2] * alpha + pv[DH:DH + 1]


def each_arrived(sel_ref, place_ref, x_ref, kv_refs, q_s, kv_s, first, count, step):
    y, x = ctx_position()
    base = (y * SIDE + x) * QB

    def body(e, carry):
        pick = sel_ref[base + e // TOPK, e % TOPK]
        owner = pick // 32

        slot = jnp.int32(0)
        for f in range(ENTRIES):
            same = (sel_ref[base + f // TOPK, f % TOPK] // 32 == owner) & (f < e)
            slot = slot + same.astype(jnp.int32)
        dy = (y - owner // SIDE + SIDE) % SIDE
        dx = (x - owner % SIDE + SIDE) % SIDE
        place = place_ref[dy * SIDE + dx]
        for i, ref in enumerate(kv_refs):
            @pl.when(place == i)
            def _(ref=ref):
                kv_s[...] = ref[slot]

        @pl.when(place >= 0)
        def _():
            q_s[...] = x_ref[e // TOPK, :, :GROUP * DH]
            step(e // TOPK)

        return carry

    lax.fori_loop(first, first + count, body, 0)


def far_kernel(n, sel_ref, place_ref, x_ref, *refs):
    kv_refs, (acc_in, ml_in, acc, ml, q_s, kv_s) = refs[:n], refs[n:]
    each_arrived(
        sel_ref, place_ref, x_ref, kv_refs, q_s, kv_s, 0, ENTRIES,
        lambda b: add_block(q_s, kv_s[...], acc, ml, b),
    )


def last_kernel(n, ahead, sel_ref, place_ref, x_ref, *refs):
    kv_refs, (acc_in, ml_in, same_ref, other_ref, acc, ml, q_s, kv_s, out_s) = refs[:n], refs[n:]
    rank = lax.axis_index("head")
    b = (rank // 2 + ahead) % QB
    core = rank % 2
    acc[0] = acc_in[b]
    ml[0] = ml_in[b]
    each_arrived(
        sel_ref, place_ref, x_ref, kv_refs, q_s, kv_s, b * TOPK, TOPK,
        lambda b: add_block(q_s, kv_s[...], acc, ml, 0),
    )
    for g in range(GROUP):
        out = (acc[0, g] * (1.0 / ml[0, g, 1:2])).astype(out_s.dtype)
        out_s[:, g * DH:(g + 1) * DH] = out.T
    half = BLK // 2
    same_ref[...] = out_s[pl.ds(pl.multiple_of(core * half, half), half), :]
    other_ref[...] = out_s[pl.ds(pl.multiple_of((1 - core) * half, half), half), :]


ACC = (QB, GROUP, DH, BLK)
ML = (QB, GROUP, 8, BLK)


def state_shapes():
    return [jax.ShapeDtypeStruct(ACC, jnp.float32), jax.ShapeDtypeStruct(ML, jnp.float32)]


def cost(blocks):
    units = int(blocks * GROUP)
    return pl.CostEstimate(
        flops=units * 4 * BLK * BLK * DH, bytes_accessed=units * BLK * DH * 2, transcendentals=units * BLK * BLK
    )


def own_call(x):
    return pl.pallas_call(
        own_kernel,
        in_specs=[VMEM],
        out_specs=[VMEM, VMEM],
        out_shape=state_shapes(),
        compiler_params=PARAMS,
        cost_estimate=cost(QB),
        name="own_blocks",
    )(x)


def far_call(sel, place, x, tiles, acc, ml):
    n = len(tiles)
    return pl.pallas_call(
        lambda *refs: far_kernel(n, *refs),
        in_specs=[SMEM, SMEM] + [VMEM] * (n + 3),
        out_specs=[VMEM, VMEM],
        out_shape=state_shapes(),
        scratch_shapes=[pltpu.VMEM((BLK, GROUP * DH), x.dtype), pltpu.VMEM((BLK, 2 * DH), x.dtype)],
        input_output_aliases={n + 3: 0, n + 4: 1},
        compiler_params=PARAMS,
        cost_estimate=cost(n * 0.75),
        name="far_blocks",
    )(sel, place, x, *tiles, acc, ml)


def last_call(ahead, sel, place, x, tiles, acc, ml):
    n = len(tiles)
    half = BLK // 2
    return pl.pallas_call(
        lambda *refs: last_kernel(n, ahead, *refs),
        in_specs=[SMEM, SMEM] + [VMEM] * (n + 3),
        out_specs=[VMEM, VMEM],
        out_shape=[jax.ShapeDtypeStruct((half, GROUP * DH), x.dtype)] * 2,
        scratch_shapes=[
            pltpu.VMEM((1,) + ACC[1:], jnp.float32),
            pltpu.VMEM((1,) + ML[1:], jnp.float32),
            pltpu.VMEM((BLK, GROUP * DH), x.dtype),
            pltpu.VMEM((BLK, 2 * DH), x.dtype),
            pltpu.VMEM((BLK, GROUP * DH), x.dtype),
        ],
        compiler_params=PARAMS,
        cost_estimate=cost(1),
        name="last_blocks",
    )(sel, place, x, *tiles, acc, ml)


def assemble_kernel(steps, *refs):
    pieces, out_ref = refs[:-1], refs[-1]
    rank = lax.axis_index("head")
    z, core = rank // 2, rank % 2
    width = GROUP * DH
    for (dz, dc), piece in zip(steps, pieces):
        sender = ((z - dz + QB) % QB) * 2 + (core + dc) % 2
        out_ref[:, pl.ds(pl.multiple_of(sender * width, width), width)] = piece[...]


def assemble_call(steps, pieces, heads):
    rows, width = pieces[0].shape
    return pl.pallas_call(
        lambda *refs: assemble_kernel(steps, *refs),
        in_specs=[VMEM] * len(pieces),
        out_specs=VMEM,
        out_shape=jax.ShapeDtypeStruct((rows, heads * width), pieces[0].dtype),
        compiler_params=PARAMS,
        name="assemble",
    )(*pieces)


def ctx_shift(value, dy, dx):
    pairs = [
        (y * SIDE + x, ((y + dy) % SIDE) * SIDE + (x + dx) % SIDE) for y in range(SIDE) for x in range(SIDE)
    ]
    return lax.ppermute(value, "ctx", pairs)


def head_shift(value, dz, dc):
    pairs = [(z * 2 + c, ((z + dz) % QB) * 2 + (c + dc) % 2) for z in range(QB) for c in range(2)]
    return lax.ppermute(value, "head", pairs)


def local(queries, span_kv, context_kv, selected):
    heads = lax.axis_size("head")
    rows = queries.shape[0]
    sel = selected[0]
    stored = context_kv[0]
    tiles = stored.reshape(stored.shape[0] // BLK, BLK, 2 * DH)

    numbers = list(range(SELF + 1))
    sent = dict(zip(numbers[:FIRST], serve_call(numbers[:FIRST], sel, tiles)))
    sent.update(zip(numbers[FIRST:], serve_call(numbers[FIRST:], sel, tiles)))
    packed = pack_call(queries, span_kv, heads)
    x = lax.all_to_all(packed, "head", split_axis=0, concat_axis=0, tiled=True)
    x = x.reshape(QB, heads * rows // QB, (GROUP + 2) * DH)

    arrived = {SELF: sent[SELF]}

    def send(number, *before):
        value = sent[number]
        if number >= FLIGHT:
            value, arrived[number - FLIGHT], *before = lax.optimization_barrier(
                (value, arrived[number - FLIGHT], *before)
            )
        arrived[number] = ctx_shift(value, *ORDER[number])
        return before

    def far(members, acc, ml):
        return far_call(sel, place_table(members), x, [arrived[i] for i in members], acc, ml)

    for number in range(2 * FLIGHT):
        send(number)
    acc, ml = own_call(x)
    acc, ml = far(GROUPS[0], acc, ml)
    for number in range(2 * FLIGHT, len(ORDER)):
        ml, = send(number, ml)
    for members in GROUPS[1:]:
        acc, ml = far(members, acc, ml)

    steps, pieces = [], []
    for dz in (2, 1, 3, 0):
        same, other = last_call(dz, sel, place_table(LAST), x, [arrived[i] for i in LAST], acc, ml)
        same, other, acc = lax.optimization_barrier((same, other, acc))
        for dc, piece in ((0, same), (1, other)):
            steps.append((dz, dc))
            pieces.append(head_shift(piece, dz, dc) if dz or dc else piece)
    return assemble_call(steps, pieces, heads)


def solution(mesh):
    placed = (
        P(("ctx", "head"), None),
        P(("ctx", "head"), None),
        P("head", "ctx", None),
        P("head", None, None),
    )
    return jax.shard_map(
        local, mesh=mesh, in_specs=placed, out_specs=P(("ctx", "head"), None), check_vma=False
    )
```

```python
import jax
import jax.numpy as jnp
import numpy as np
from jax import lax
from jax.experimental import pallas as pl
from jax.experimental.pallas import tpu as pltpu
from jax.sharding import PartitionSpec as P

BLK = 512
CAP = 2
DH = 128
GROUP = 4
TOPK = 3
QB = 4
ENTRIES = QB * TOPK
SIDE = 4
ONES = 16
C = DH ** -0.5 * 1.4426950408889634

ORDER = [
    (0, 1), (0, 3), (1, 0), (3, 0), (2, 2), (1, 1), (3, 3), (1, 3),
    (3, 1), (1, 2), (3, 2), (2, 1), (2, 3), (0, 2), (2, 0),
]
SELF = len(ORDER)
FIRST = 5
GROUPS = [[SELF, 0, 1], [2, 3, 4], [5, 6, 7, 8, 9], [10, 11]]
LAST = [12, 13, 14]
FLIGHT = 5

VMEM = pl.BlockSpec(memory_space=pltpu.VMEM)
SMEM = pl.BlockSpec(memory_space=pltpu.SMEM)
HBM = pl.BlockSpec(memory_space=pltpu.HBM)
WIDE = pltpu.CompilerParams(vmem_limit_bytes=54 * 1024 * 1024)
PARAMS = pltpu.CompilerParams(vmem_limit_bytes=20 * 1024 * 1024)


def place_table(members):
    table = np.full((SIDE * SIDE,), -1, np.int32)
    for place, number in enumerate(members):
        dy, dx = (0, 0) if number == SELF else ORDER[number]
        table[dy * SIDE + dx] = place
    return jnp.asarray(table)


def ctx_position():
    rank = lax.axis_index("ctx")
    return rank // SIDE, rank % SIDE


def serve_start(members, sel_ref, tiles_ref, outs, stage, sem, sem_out):
    y, x = ctx_position()
    me = y * SIDE + x
    copies = []
    for out, number in zip(outs, members):
        dy, dx = (0, 0) if number == SELF else ORDER[number]
        asker = ((y + dy) % SIDE) * SIDE + (x + dx) % SIDE
        found = jnp.int32(0)
        which = [jnp.int32(0)] * CAP
        for e in range(ENTRIES):
            pick = sel_ref[e % TOPK, 0, asker * QB + e // TOPK]
            hit = pick // 32 == me
            for s in range(CAP):
                which[s] = jnp.where(hit & (found == s), pick % 32, which[s])
            found = found + hit.astype(jnp.int32)
        for s in range(CAP):
            place = len(copies)
            if stage is None:
                copies.append(pltpu.make_async_copy(tiles_ref.at[which[s]], out.at[s], sem.at[place]))
                copies[-1].start()
                continue
            copy = pltpu.make_async_copy(tiles_ref.at[which[s]], stage.at[place], sem.at[place])
            copy.start()
            copies.append((copy, pltpu.make_async_copy(stage.at[place], out.at[s], sem_out.at[place])))
    return copies


def pass_on(copies):
    for copy, onward in copies:
        copy.wait()
        onward.start()
    for _, onward in copies:
        onward.wait()


def serve_kernel(members, sel_ref, tiles_ref, *refs):
    pass_on(serve_start(members, sel_ref, tiles_ref, refs[:-3], *refs[-3:]))


def first_kernel(members, heads, sel_ref, tiles_ref, q_ref, s_ref, *refs):
    outs, (packed_ref, sem, q_sem, s_sem) = refs[:-4], refs[-4:]
    width = GROUP * DH
    inward = []
    for h in range(heads):
        inward.append(
            pltpu.make_async_copy(
                q_ref.at[:, pl.ds(h * width, width)], packed_ref.at[h, :, pl.ds(0, width)], q_sem.at[h]
            )
        )
        inward.append(
            pltpu.make_async_copy(
                s_ref.at[:, pl.ds(h * 2 * DH, 2 * DH)], packed_ref.at[h, :, pl.ds(width, 2 * DH)], s_sem.at[h]
            )
        )
    for copy in inward:
        copy.start()
    copies = serve_start(members, sel_ref, tiles_ref, outs, None, sem, None)
    for copy in inward + copies:
        copy.wait()


def stage_shapes(n, dtype):
    return [
        pltpu.VMEM((CAP * n, BLK, 2 * DH), dtype),
        pltpu.SemaphoreType.DMA((CAP * n,)),
        pltpu.SemaphoreType.DMA((CAP * n,)),
    ]


def serve_call(members, sel, tiles):
    n = len(members)
    return pl.pallas_call(
        lambda *refs: serve_kernel(members, *refs),
        in_specs=[SMEM, HBM],
        out_specs=[HBM] * n,
        out_shape=[jax.ShapeDtypeStruct((CAP, BLK, 2 * DH), tiles.dtype)] * n,
        scratch_shapes=stage_shapes(n, tiles.dtype),
        compiler_params=WIDE,
        name="serve",
    )(sel, tiles)


def first_call(members, sel, tiles, queries, span_kv, heads):
    n = len(members)
    packed = (heads, queries.shape[0], (GROUP + 2) * DH)
    return pl.pallas_call(
        lambda *refs: first_kernel(members, heads, *refs),
        in_specs=[SMEM, HBM, HBM, HBM],
        out_specs=[VMEM] * (n + 1),
        out_shape=[jax.ShapeDtypeStruct((CAP, BLK, 2 * DH), tiles.dtype)] * n
        + [jax.ShapeDtypeStruct(packed, queries.dtype)],
        scratch_shapes=[
            pltpu.SemaphoreType.DMA((CAP * n,)),
            pltpu.SemaphoreType.DMA((heads,)),
            pltpu.SemaphoreType.DMA((heads,)),
        ],
        compiler_params=WIDE,
        name="first",
    )(sel, tiles, queries, span_kv)


def values_t(v):
    return jnp.concatenate([v.T, jnp.ones((ONES, BLK), v.dtype)], axis=0)


def scores_t(k, q):
    return lax.dot_general(k, q, (((1,), (1,)), ((), ())), preferred_element_type=jnp.float32)


def own_kernel(x_ref, acc, ml):
    def body(b, carry):
        k = x_ref[b, :, GROUP * DH:(GROUP + 1) * DH]
        vt = values_t(x_ref[b, :, (GROUP + 1) * DH:])
        key = lax.broadcasted_iota(jnp.int32, (BLK, BLK), 0)
        query = lax.broadcasted_iota(jnp.int32, (BLK, BLK), 1)
        found = [scores_t(k, x_ref[b, :, g * DH:(g + 1) * DH]) for g in range(GROUP)]
        for g in range(GROUP):
            s = jnp.where(key <= query, found[g], -jnp.inf)
            m = jnp.max(s, axis=0, keepdims=True)
            p = jnp.exp2((s - m) * C).astype(jnp.bfloat16)
            pv = jnp.dot(vt, p, preferred_element_type=jnp.float32)
            acc[b, g] = pv[:DH]
            ml[b, g, 0:1] = m
            ml[b, g, 1:2] = pv[DH:DH + 1]
        return carry

    lax.fori_loop(0, QB, body, 0)


def add_block(q, kv, acc, ml, at):
    k = kv[:, :DH]
    vt = values_t(kv[:, DH:])
    found = [scores_t(k, q[:, g * DH:(g + 1) * DH]) for g in range(GROUP)]
    for g in range(GROUP):
        s = found[g]
        m_old = ml[at, g, 0:1]
        m = jnp.maximum(m_old, jnp.max(s, axis=0, keepdims=True))
        p = jnp.exp2((s - m) * C).astype(jnp.bfloat16)
        alpha = jnp.exp2((m_old - m) * C)
        pv = jnp.dot(vt, p, preferred_element_type=jnp.float32)
        acc[at, g] = acc[at, g] * alpha + pv[:DH]
        ml[at, g, 0:1] = m
        ml[at, g, 1:2] = ml[at, g, 1:2] * alpha + pv[DH:DH + 1]


def each_arrived(sel_ref, place_ref, x_ref, kv_refs, scratch, first, count, step):
    q_s, kv_s, kv_all, which_s, sem = scratch
    y, x = ctx_position()
    base = (y * SIDE + x) * QB

    def fetch(e, found):
        pick = sel_ref[e % TOPK, 0, base + e // TOPK]
        owner = pick // 32
        slot = jnp.int32(0)
        for f in range(ENTRIES):
            same = (sel_ref[f % TOPK, 0, base + f // TOPK] // 32 == owner) & (f < e)
            slot = slot + same.astype(jnp.int32)
        dy = (y - owner // SIDE + SIDE) % SIDE
        dx = (x - owner % SIDE + SIDE) % SIDE
        place = place_ref[dy * SIDE + dx]
        for i, ref in enumerate(kv_refs):
            @pl.when(place == i)
            def _(ref=ref):
                pltpu.make_async_copy(ref.at[slot], kv_all.at[found], sem.at[found]).start()

        @pl.when(place >= 0)
        def _():
            which_s[found] = e // TOPK

        return found + (place >= 0).astype(jnp.int32)

    def work(n, carry):
        b = which_s[n]
        q_s[...] = x_ref[b, :, :GROUP * DH]
        pltpu.make_async_copy(kv_refs[0].at[0], kv_all.at[n], sem.at[n]).wait()
        kv_s[...] = kv_all[n]
        step(b, q_s, kv_s[...])
        return carry

    lax.fori_loop(0, lax.fori_loop(first, first + count, fetch, jnp.int32(0)), work, 0)


def arrived_scratch(n, dtype):
    return [
        pltpu.VMEM((BLK, GROUP * DH), dtype),
        pltpu.VMEM((BLK, 2 * DH), dtype),
        pltpu.VMEM((n, BLK, 2 * DH), dtype),
        pltpu.SMEM((n,), jnp.int32),
        pltpu.SemaphoreType.DMA((n,)),
    ]


def far_kernel(n, sel_ref, place_ref, x_ref, *refs):
    kv_refs, (acc_in, ml_in, acc, ml), scratch = refs[:n], refs[n:n + 4], refs[n + 4:]
    acc[...] = acc_in[...]
    ml[...] = ml_in[...]
    each_arrived(
        sel_ref, place_ref, x_ref, kv_refs, scratch, 0, ENTRIES,
        lambda b, q, kv: add_block(q, kv, acc, ml, b),
    )


def last_kernel(n, aheads, sel_ref, place_ref, x_ref, *refs):
    kv_refs, refs = refs[:n], refs[n:]
    acc_in, ml_in, refs = refs[0], refs[1], refs[2:]
    outs, (acc, ml, out_s), scratch = refs[:2 * len(aheads)], refs[2 * len(aheads):][:3], refs[2 * len(aheads) + 3:]
    rank = lax.axis_index("head")
    core = rank % 2
    half = BLK // 2
    for i, ahead in enumerate(aheads):
        b = (rank // 2 + ahead) % QB
        acc[0] = acc_in[b]
        ml[0] = ml_in[b]
        each_arrived(
            sel_ref, place_ref, x_ref, kv_refs, scratch, b * TOPK, TOPK,
            lambda b, q, kv: add_block(q, kv, acc, ml, 0),
        )
        for g in range(GROUP):
            out = (acc[0, g] * (1.0 / ml[0, g, 1:2])).astype(out_s.dtype)
            out_s[:, g * DH:(g + 1) * DH] = out.T
        outs[2 * i][...] = out_s[pl.ds(pl.multiple_of(core * half, half), half), :]
        outs[2 * i + 1][...] = out_s[pl.ds(pl.multiple_of((1 - core) * half, half), half), :]


ACC = (QB, GROUP, DH, BLK)
ML = (QB, GROUP, 8, BLK)


def state_shapes():
    return [jax.ShapeDtypeStruct(ACC, jnp.float32), jax.ShapeDtypeStruct(ML, jnp.float32)]


def cost(blocks):
    units = int(blocks * GROUP)
    return pl.CostEstimate(
        flops=units * 4 * BLK * BLK * DH, bytes_accessed=units * BLK * DH * 2, transcendentals=units * BLK * BLK
    )


def own_call(x):
    return pl.pallas_call(
        own_kernel,
        in_specs=[VMEM],
        out_specs=[VMEM, VMEM],
        out_shape=state_shapes(),
        compiler_params=PARAMS,
        cost_estimate=cost(QB),
        name="own_blocks",
    )(x)


def far_call(sel, place, x, tiles, acc, ml):
    n = len(tiles)
    return pl.pallas_call(
        lambda *refs: far_kernel(n, *refs),
        in_specs=[SMEM, SMEM, VMEM] + [HBM] * n + [VMEM] * 2,
        out_specs=[VMEM, VMEM],
        out_shape=state_shapes(),
        scratch_shapes=arrived_scratch(CAP * n, x.dtype),
        compiler_params=PARAMS,
        cost_estimate=cost(n * 0.75),
        name="far_blocks",
    )(sel, place, x, *tiles, acc, ml)


def last_call(aheads, sel, place, x, tiles, acc, ml):
    n = len(tiles)
    half = BLK // 2
    return pl.pallas_call(
        lambda *refs: last_kernel(n, aheads, *refs),
        in_specs=[SMEM, SMEM, VMEM] + [HBM] * n + [VMEM] * 2,
        out_specs=[VMEM] * (2 * len(aheads)),
        out_shape=[jax.ShapeDtypeStruct((half, GROUP * DH), x.dtype)] * (2 * len(aheads)),
        scratch_shapes=[
            pltpu.VMEM((1,) + ACC[1:], jnp.float32),
            pltpu.VMEM((1,) + ML[1:], jnp.float32),
            pltpu.VMEM((BLK, GROUP * DH), x.dtype),
        ] + arrived_scratch(TOPK, x.dtype),
        compiler_params=PARAMS,
        cost_estimate=cost(1),
        name="last_blocks",
    )(sel, place, x, *tiles, acc, ml)


def assemble_kernel(steps, *refs):
    pieces, out_ref = refs[:-1], refs[-1]
    rank = lax.axis_index("head")
    z, core = rank // 2, rank % 2
    width = GROUP * DH
    for (dz, dc), piece in zip(steps, pieces):
        sender = ((z - dz + QB) % QB) * 2 + (core + dc) % 2
        out_ref[:, pl.ds(pl.multiple_of(sender * width, width), width)] = piece[...]


def assemble_call(steps, pieces, heads):
    rows, width = pieces[0].shape
    return pl.pallas_call(
        lambda *refs: assemble_kernel(steps, *refs),
        in_specs=[VMEM] * len(pieces),
        out_specs=VMEM,
        out_shape=jax.ShapeDtypeStruct((rows, heads * width), pieces[0].dtype),
        compiler_params=PARAMS,
        name="assemble",
    )(*pieces)


def ctx_shift(value, dy, dx):
    pairs = [
        (y * SIDE + x, ((y + dy) % SIDE) * SIDE + (x + dx) % SIDE) for y in range(SIDE) for x in range(SIDE)
    ]
    return lax.ppermute(value, "ctx", pairs)


def head_shift(value, dz, dc):
    pairs = [(z * 2 + c, ((z + dz) % QB) * 2 + (c + dc) % 2) for z in range(QB) for c in range(2)]
    return lax.ppermute(value, "head", pairs)


def local(queries, span_kv, context_kv, selected):
    heads = lax.axis_size("head")
    rows = queries.shape[0]
    sel = selected.transpose(2, 0, 1)
    stored = context_kv[0]
    tiles = stored.reshape(stored.shape[0] // BLK, BLK, 2 * DH)

    numbers = list(range(SELF + 1))
    *begin, packed = first_call(numbers[:FIRST], sel, tiles, queries, span_kv, heads)
    sent = dict(zip(numbers[:FIRST], begin))
    sent.update(zip(numbers[FIRST:], serve_call(numbers[FIRST:], sel, tiles)))
    x = lax.all_to_all(packed, "head", split_axis=0, concat_axis=0, tiled=True)
    x = x.reshape(QB, heads * rows // QB, (GROUP + 2) * DH)

    arrived = {SELF: sent[SELF]}

    def send(number, *before):
        value = sent[number]
        if number >= FLIGHT:
            value, arrived[number - FLIGHT], *before = lax.optimization_barrier(
                (value, arrived[number - FLIGHT], *before)
            )
        arrived[number] = ctx_shift(value, *ORDER[number])
        return before

    def far(members, acc, ml):
        return far_call(sel, place_table(members), x, [arrived[i] for i in members], acc, ml)

    for number in range(2 * FLIGHT):
        send(number)
    acc, ml = own_call(x)
    for number in (10, 11):
        ml, = send(number, ml)
    acc, ml = far(GROUPS[0], acc, ml)
    for number in (12, 13):
        ml, = send(number, ml)
    acc, ml = far(GROUPS[1], acc, ml)
    ml, = send(14, ml)
    for members in GROUPS[2:]:
        acc, ml = far(members, acc, ml)

    ready = {}
    for aheads in ((2,), (1, 3, 0)):
        outs = last_call(aheads, sel, place_table(LAST), x, [arrived[i] for i in LAST], acc, ml)
        *outs, acc = lax.optimization_barrier((*outs, acc))
        for i, dz in enumerate(aheads):
            for dc in range(2):
                ready[dz, dc] = outs[2 * i + dc]
    steps = [(2, 0), (2, 1), (1, 0), (3, 0), (1, 1), (3, 1), (0, 1)]
    pieces = []
    for number, step in enumerate(steps):
        value = ready[step]
        if number >= FLIGHT:
            value, pieces[number - FLIGHT] = lax.optimization_barrier((value, pieces[number - FLIGHT]))
        pieces.append(head_shift(value, *step))
    steps.append((0, 0))
    pieces.append(ready[0, 0])
    return assemble_call(steps, pieces, heads)


def solution(mesh):
    placed = (
        P(("ctx", "head"), None),
        P(("ctx", "head"), None),
        P("head", "ctx", None),
        P("head", None, None),
    )
    return jax.shard_map(
        local, mesh=mesh, in_specs=placed, out_specs=P(("ctx", "head"), None), check_vma=False
    )
```

```python
import jax
import jax.numpy as jnp
import numpy as np
from jax import lax
from jax.experimental import pallas as pl
from jax.experimental.pallas import tpu as pltpu
from jax.sharding import PartitionSpec as P

BLK = 512
CAP = 2
DH = 128
GROUP = 4
TOPK = 3
QB = 4
ENTRIES = QB * TOPK
SIDE = 4
RANGE_BITS = 5
ONES = 16
C = DH ** -0.5 * 1.4426950408889634

ORDER = [
    (0, 1), (0, 3), (1, 0), (3, 0), (2, 2), (1, 1), (3, 3), (1, 3),
    (3, 1), (1, 2), (3, 2), (2, 1), (2, 3), (0, 2), (2, 0),
]
SELF = len(ORDER)
FIRST = 5
GROUPS = [[SELF, 0, 1], [2, 3, 4], [5, 6, 7, 8, 9], [10, 11]]
LAST = [12, 13, 14]
FLIGHT = 5

VMEM = pl.BlockSpec(memory_space=pltpu.VMEM)
SMEM = pl.BlockSpec(memory_space=pltpu.SMEM)
HBM = pl.BlockSpec(memory_space=pltpu.HBM)
WIDE = pltpu.CompilerParams(vmem_limit_bytes=54 * 1024 * 1024)
PARAMS = pltpu.CompilerParams(vmem_limit_bytes=20 * 1024 * 1024)


def place_table(members):
    table = np.full((SIDE * SIDE,), -1, np.int32)
    for place, number in enumerate(members):
        dy, dx = (0, 0) if number == SELF else ORDER[number]
        table[dy * SIDE + dx] = place
    return jnp.asarray(table)


def ctx_position():
    rank = lax.axis_index("ctx")
    return rank >> 2, rank & (SIDE - 1)


def serve_start(members, sel_ref, tiles_ref, outs, stage, sem, sem_out):
    y, x = ctx_position()
    me = y * SIDE + x
    copies = []
    for out, number in zip(outs, members):
        dy, dx = (0, 0) if number == SELF else ORDER[number]
        asker = ((y + dy) & (SIDE - 1)) * SIDE + ((x + dx) & (SIDE - 1))
        found = jnp.int32(0)
        which = [jnp.int32(0)] * CAP
        for e in range(ENTRIES):
            pick = sel_ref[e % TOPK, 0, asker * QB + e // TOPK]
            hit = pick >> RANGE_BITS == me
            for s in range(CAP):
                which[s] = jnp.where(hit & (found == s), pick & (2 ** RANGE_BITS - 1), which[s])
            found = found + hit.astype(jnp.int32)
        for s in range(CAP):
            place = len(copies)
            if stage is None:
                copies.append(pltpu.make_async_copy(tiles_ref.at[which[s]], out.at[s], sem.at[place]))
                copies[-1].start()
                continue
            copy = pltpu.make_async_copy(tiles_ref.at[which[s]], stage.at[place], sem.at[place])
            copy.start()
            copies.append((copy, pltpu.make_async_copy(stage.at[place], out.at[s], sem_out.at[place])))
    return copies


def pass_on(copies):
    for copy, onward in copies:
        copy.wait()
        onward.start()
    for _, onward in copies:
        onward.wait()


def serve_kernel(members, sel_ref, tiles_ref, *refs):
    pass_on(serve_start(members, sel_ref, tiles_ref, refs[:-3], *refs[-3:]))


def first_kernel(members, heads, sel_ref, tiles_ref, q_ref, s_ref, *refs):
    outs, (packed_ref, sem, q_sem, s_sem) = refs[:-4], refs[-4:]
    width = GROUP * DH
    inward = []
    for h in range(heads):
        inward.append(
            pltpu.make_async_copy(
                q_ref.at[:, pl.ds(h * width, width)], packed_ref.at[h, :, pl.ds(0, width)], q_sem.at[h]
            )
        )
        inward.append(
            pltpu.make_async_copy(
                s_ref.at[:, pl.ds(h * 2 * DH, 2 * DH)], packed_ref.at[h, :, pl.ds(width, 2 * DH)], s_sem.at[h]
            )
        )
    for copy in inward:
        copy.start()
    copies = serve_start(members, sel_ref, tiles_ref, outs, None, sem, None)
    for copy in inward + copies:
        copy.wait()


def stage_shapes(n, dtype):
    return [
        pltpu.VMEM((CAP * n, BLK, 2 * DH), dtype),
        pltpu.SemaphoreType.DMA((CAP * n,)),
        pltpu.SemaphoreType.DMA((CAP * n,)),
    ]


def serve_call(members, sel, tiles):
    n = len(members)
    return pl.pallas_call(
        lambda *refs: serve_kernel(members, *refs),
        in_specs=[SMEM, HBM],
        out_specs=[HBM] * n,
        out_shape=[jax.ShapeDtypeStruct((CAP, BLK, 2 * DH), tiles.dtype)] * n,
        scratch_shapes=stage_shapes(n, tiles.dtype),
        compiler_params=WIDE,
        name="serve",
    )(sel, tiles)


def first_call(members, sel, tiles, queries, span_kv, heads):
    n = len(members)
    packed = (heads, queries.shape[0], (GROUP + 2) * DH)
    return pl.pallas_call(
        lambda *refs: first_kernel(members, heads, *refs),
        in_specs=[SMEM, HBM, HBM, HBM],
        out_specs=[VMEM] * (n + 1),
        out_shape=[jax.ShapeDtypeStruct((CAP, BLK, 2 * DH), tiles.dtype)] * n
        + [jax.ShapeDtypeStruct(packed, queries.dtype)],
        scratch_shapes=[
            pltpu.SemaphoreType.DMA((CAP * n,)),
            pltpu.SemaphoreType.DMA((heads,)),
            pltpu.SemaphoreType.DMA((heads,)),
        ],
        compiler_params=WIDE,
        name="first",
    )(sel, tiles, queries, span_kv)


def values_t(v):
    return jnp.concatenate([v.T, jnp.ones((ONES, BLK), v.dtype)], axis=0)


def scores_t(k, q):
    return lax.dot_general(k, q, (((1,), (1,)), ((), ())), preferred_element_type=jnp.float32)


def own_kernel(x_ref, acc, ml):
    def body(b, carry):
        k = x_ref[b, :, GROUP * DH:(GROUP + 1) * DH]
        vt = values_t(x_ref[b, :, (GROUP + 1) * DH:])
        key = lax.broadcasted_iota(jnp.int32, (BLK, BLK), 0)
        query = lax.broadcasted_iota(jnp.int32, (BLK, BLK), 1)
        found = [scores_t(k, x_ref[b, :, g * DH:(g + 1) * DH]) for g in range(GROUP)]
        for g in range(GROUP):
            s = jnp.where(key <= query, found[g], -jnp.inf)
            m = jnp.max(s, axis=0, keepdims=True)
            p = jnp.exp2((s - m) * C).astype(jnp.bfloat16)
            pv = jnp.dot(vt, p, preferred_element_type=jnp.float32)
            acc[b, g] = pv[:DH]
            ml[b, g, 0:1] = m
            ml[b, g, 1:2] = pv[DH:DH + 1]
        return carry

    lax.fori_loop(0, QB, body, 0)


def add_block(q, kv, acc, ml, at):
    k = kv[:, :DH]
    vt = values_t(kv[:, DH:])
    found = [scores_t(k, q[:, g * DH:(g + 1) * DH]) for g in range(GROUP)]
    for g in range(GROUP):
        s = found[g]
        m_old = ml[at, g, 0:1]
        m = jnp.maximum(m_old, jnp.max(s, axis=0, keepdims=True))
        p = jnp.exp2((s - m) * C).astype(jnp.bfloat16)
        alpha = jnp.exp2((m_old - m) * C)
        pv = jnp.dot(vt, p, preferred_element_type=jnp.float32)
        acc[at, g] = acc[at, g] * alpha + pv[:DH]
        ml[at, g, 0:1] = m
        ml[at, g, 1:2] = ml[at, g, 1:2] * alpha + pv[DH:DH + 1]


def each_arrived(sel_ref, place_ref, x_ref, kv_refs, scratch, first, count, step):
    q_s, kv_s, kv_all, which_s, sem = scratch
    y, x = ctx_position()
    base = (y * SIDE + x) * QB

    def pick_of(e):
        return sel_ref[lax.rem(e, jnp.int32(TOPK)), 0, base + lax.div(e, jnp.int32(TOPK))]

    def fetch(e, found):
        owner = pick_of(e) >> RANGE_BITS
        dy = (y - (owner >> 2)) & (SIDE - 1)
        dx = (x - owner) & (SIDE - 1)
        place = place_ref[dy * SIDE + dx]

        @pl.when(place >= 0)
        def _():
            slot = jnp.int32(0)
            for f in range(ENTRIES):
                same = (pick_of(jnp.int32(f)) >> RANGE_BITS == owner) & (f < e)
                slot = slot + same.astype(jnp.int32)
            for i, ref in enumerate(kv_refs):
                @pl.when(place == i)
                def _(ref=ref):
                    pltpu.make_async_copy(ref.at[slot], kv_all.at[found], sem.at[found]).start()

            which_s[found] = lax.div(e, jnp.int32(TOPK))

        return found + (place >= 0).astype(jnp.int32)

    def work(n, carry):
        b = which_s[n]
        q_s[...] = x_ref[b, :, :GROUP * DH]
        pltpu.make_async_copy(kv_refs[0].at[0], kv_all.at[n], sem.at[n]).wait()
        kv_s[...] = kv_all[n]
        step(b, q_s, kv_s[...])
        return carry

    lax.fori_loop(0, lax.fori_loop(first, first + count, fetch, jnp.int32(0)), work, 0)


def arrived_scratch(n, dtype):
    return [
        pltpu.VMEM((BLK, GROUP * DH), dtype),
        pltpu.VMEM((BLK, 2 * DH), dtype),
        pltpu.VMEM((n, BLK, 2 * DH), dtype),
        pltpu.SMEM((n,), jnp.int32),
        pltpu.SemaphoreType.DMA((n,)),
    ]


def far_kernel(n, sel_ref, place_ref, x_ref, *refs):
    kv_refs, (acc_in, ml_in, acc, ml), scratch = refs[:n], refs[n:n + 4], refs[n + 4:]
    acc[...] = acc_in[...]
    ml[...] = ml_in[...]
    each_arrived(
        sel_ref, place_ref, x_ref, kv_refs, scratch, 0, ENTRIES,
        lambda b, q, kv: add_block(q, kv, acc, ml, b),
    )


def last_kernel(n, aheads, sel_ref, place_ref, x_ref, *refs):
    kv_refs, refs = refs[:n], refs[n:]
    acc_in, ml_in, refs = refs[0], refs[1], refs[2:]
    outs, (acc, ml, out_s), scratch = refs[:2 * len(aheads)], refs[2 * len(aheads):][:3], refs[2 * len(aheads) + 3:]
    rank = lax.axis_index("head")
    core = rank & 1
    half = BLK // 2
    for i, ahead in enumerate(aheads):
        b = ((rank >> 1) + ahead) & (QB - 1)
        acc[0] = acc_in[b]
        ml[0] = ml_in[b]
        each_arrived(
            sel_ref, place_ref, x_ref, kv_refs, scratch, b * TOPK, TOPK,
            lambda b, q, kv: add_block(q, kv, acc, ml, 0),
        )
        for g in range(GROUP):
            out = (acc[0, g] * (1.0 / ml[0, g, 1:2])).astype(out_s.dtype)
            out_s[:, g * DH:(g + 1) * DH] = out.T
        outs[2 * i][...] = out_s[pl.ds(pl.multiple_of(core * half, half), half), :]
        outs[2 * i + 1][...] = out_s[pl.ds(pl.multiple_of((1 - core) * half, half), half), :]


ACC = (QB, GROUP, DH, BLK)
ML = (QB, GROUP, 8, BLK)


def state_shapes():
    return [jax.ShapeDtypeStruct(ACC, jnp.float32), jax.ShapeDtypeStruct(ML, jnp.float32)]


def cost(blocks):
    units = int(blocks * GROUP)
    return pl.CostEstimate(
        flops=units * 4 * BLK * BLK * DH, bytes_accessed=units * BLK * DH * 2, transcendentals=units * BLK * BLK
    )


def own_call(x):
    return pl.pallas_call(
        own_kernel,
        in_specs=[VMEM],
        out_specs=[VMEM, VMEM],
        out_shape=state_shapes(),
        compiler_params=PARAMS,
        cost_estimate=cost(QB),
        name="own_blocks",
    )(x)


def far_call(sel, place, x, tiles, acc, ml):
    n = len(tiles)
    return pl.pallas_call(
        lambda *refs: far_kernel(n, *refs),
        in_specs=[SMEM, SMEM, VMEM] + [HBM] * n + [VMEM] * 2,
        out_specs=[VMEM, VMEM],
        out_shape=state_shapes(),
        scratch_shapes=arrived_scratch(CAP * n, x.dtype),
        compiler_params=PARAMS,
        cost_estimate=cost(n * 0.75),
        name="far_blocks",
    )(sel, place, x, *tiles, acc, ml)


def last_call(aheads, sel, place, x, tiles, acc, ml):
    n = len(tiles)
    half = BLK // 2
    return pl.pallas_call(
        lambda *refs: last_kernel(n, aheads, *refs),
        in_specs=[SMEM, SMEM, VMEM] + [HBM] * n + [VMEM] * 2,
        out_specs=[VMEM] * (2 * len(aheads)),
        out_shape=[jax.ShapeDtypeStruct((half, GROUP * DH), x.dtype)] * (2 * len(aheads)),
        scratch_shapes=[
            pltpu.VMEM((1,) + ACC[1:], jnp.float32),
            pltpu.VMEM((1,) + ML[1:], jnp.float32),
            pltpu.VMEM((BLK, GROUP * DH), x.dtype),
        ] + arrived_scratch(TOPK, x.dtype),
        compiler_params=PARAMS,
        cost_estimate=cost(1),
        name="last_blocks",
    )(sel, place, x, *tiles, acc, ml)


def assemble_kernel(steps, *refs):
    pieces, out_ref = refs[:-1], refs[-1]
    rank = lax.axis_index("head")
    z, core = rank // 2, rank % 2
    width = GROUP * DH
    for (dz, dc), piece in zip(steps, pieces):
        sender = ((z - dz + QB) % QB) * 2 + (core + dc) % 2
        out_ref[:, pl.ds(pl.multiple_of(sender * width, width), width)] = piece[...]


def assemble_call(steps, pieces, heads):
    rows, width = pieces[0].shape
    return pl.pallas_call(
        lambda *refs: assemble_kernel(steps, *refs),
        in_specs=[VMEM] * len(pieces),
        out_specs=VMEM,
        out_shape=jax.ShapeDtypeStruct((rows, heads * width), pieces[0].dtype),
        compiler_params=PARAMS,
        name="assemble",
    )(*pieces)


def ctx_shift(value, dy, dx):
    pairs = [
        (y * SIDE + x, ((y + dy) % SIDE) * SIDE + (x + dx) % SIDE) for y in range(SIDE) for x in range(SIDE)
    ]
    return lax.ppermute(value, "ctx", pairs)


def head_shift(value, dz, dc):
    pairs = [(z * 2 + c, ((z + dz) % QB) * 2 + (c + dc) % 2) for z in range(QB) for c in range(2)]
    return lax.ppermute(value, "head", pairs)


def local(queries, span_kv, context_kv, selected):
    heads = lax.axis_size("head")
    rows = queries.shape[0]
    sel = selected.transpose(2, 0, 1)
    stored = context_kv[0]
    tiles = stored.reshape(stored.shape[0] // BLK, BLK, 2 * DH)

    numbers = list(range(SELF + 1))
    *begin, packed = first_call(numbers[:FIRST], sel, tiles, queries, span_kv, heads)
    sent = dict(zip(numbers[:FIRST], begin))
    sent.update(zip(numbers[FIRST:], serve_call(numbers[FIRST:], sel, tiles)))
    x = lax.all_to_all(packed, "head", split_axis=0, concat_axis=0, tiled=True)
    x = x.reshape(QB, heads * rows // QB, (GROUP + 2) * DH)

    arrived = {SELF: sent[SELF]}

    def send(number, *before):
        value = sent[number]
        if number >= FLIGHT:
            value, arrived[number - FLIGHT], *before = lax.optimization_barrier(
                (value, arrived[number - FLIGHT], *before)
            )
        arrived[number] = ctx_shift(value, *ORDER[number])
        return before

    def far(members, acc, ml):
        return far_call(sel, place_table(members), x, [arrived[i] for i in members], acc, ml)

    for number in range(2 * FLIGHT):
        send(number)
    acc, ml = own_call(x)
    for number in (10, 11):
        ml, = send(number, ml)
    acc, ml = far(GROUPS[0], acc, ml)
    for number in (12, 13):
        ml, = send(number, ml)
    acc, ml = far(GROUPS[1], acc, ml)
    ml, = send(14, ml)
    for members in GROUPS[2:]:
        acc, ml = far(members, acc, ml)

    ready = {}
    for aheads in ((2,), (1, 3, 0)):
        outs = last_call(aheads, sel, place_table(LAST), x, [arrived[i] for i in LAST], acc, ml)
        *outs, acc = lax.optimization_barrier((*outs, acc))
        for i, dz in enumerate(aheads):
            for dc in range(2):
                ready[dz, dc] = outs[2 * i + dc]
    steps = [(2, 0), (2, 1), (1, 0), (3, 0), (1, 1), (3, 1), (0, 1)]
    pieces = []
    for number, step in enumerate(steps):
        value = ready[step]
        if number >= FLIGHT:
            value, pieces[number - FLIGHT] = lax.optimization_barrier((value, pieces[number - FLIGHT]))
        pieces.append(head_shift(value, *step))
    steps.append((0, 0))
    pieces.append(ready[0, 0])
    return assemble_call(steps, pieces, heads)


def solution(mesh):
    placed = (
        P(("ctx", "head"), None),
        P(("ctx", "head"), None),
        P("head", "ctx", None),
        P("head", None, None),
    )
    return jax.shard_map(
        local, mesh=mesh, in_specs=placed, out_specs=P(("ctx", "head"), None), check_vma=False
    )
```
